32 devices in a mesh: dp: 8 (over z, core), space: 4 (over y, x).
Axes of the slice: x: 2, y: 2, z: 4, core: 2. Of those that a mesh axis runs over, the one named last changes fastest.
Arguments:
- decoder_input: bfloat16 [8, 64, 8, 16, 128], P('dp', None, 'space'), may hold values from -6 to 6
- cotangent: bfloat16 [8, 64, 8, 16, 128], P('dp', None, 'space'), may hold values from -6 to 6
- encoder_input: bfloat16 [8, 64, 8, 16, 128], P('dp', None, 'space'), may hold values from -6 to 6
- decoder_weights: bfloat16 [2, 27, 4096], replicated, may hold values from -0.15625 to 0.15625
- other_grads: bfloat16 [8, 4, 12, 27, 4096], P('dp', 'space'), may hold values from -384 to 384
- assignment: int32 [12], replicated, may hold values from 0 to 15, as said below
- moment_first: float32 [16, 27, 4096], P('dp', None, 'space'), may hold values from -4 to 4
- moment_second: float32 [16, 27, 4096], P('dp', None, 'space'), may hold values from 0.02 to 2
- master_weights: float32 [16, 27, 4096], P('dp', None, 'space'), may hold values from -0.15625 to 0.15625
Outputs:
- input_grad: bfloat16 [8, 64, 8, 16, 128], P('dp', None, 'space')
- encoder_out: bfloat16 [8, 64, 8, 16, 128], P('dp', None, 'space')
- new_params: bfloat16 [12, 27, 4096], replicated
- new_first: float32 [16, 27, 4096], P('dp', None, 'space')
- new_second: float32 [16, 27, 4096], P('dp', None, 'space')
- new_master: float32 [16, 27, 4096], P('dp', None, 'space')
The draws below stay inside these ranges and needn't reach their ends.
Inputs may be any that keep to these rules, and one draw needn't show every extreme that they name: `assignment`: the values are distinct; value j places the tensor with owner j // 2 in that owner's slot j % 2; some owner holds 2 tensors.
All inputs are finite; a program needn't handle non-finite values.
Results may differ from the reference program's by a relative error of at most 0.005.
Values may be sent and summed in bfloat16 or wider, within the bound.
A program may use at most 128 MiB of HBM per device.

```python
import math
import jax
import jax.numpy as jnp
from jax import lax

C = 64
CX = 2
NY = 16
NZ = 128
NT = 12
SLOTS = 2
NX = 8
ALL_SLOTS = 16
N_DP = 8
N_SPACE = 4


def draw_assignment(key, part):
    total_slots = N_DP * SLOTS
    key_owner, key_order, key_shuffle = jax.random.split(key, 3)
    owner = jax.random.randint(key_owner, (), 0, N_DP)
    order = jax.random.permutation(key_order, total_slots)
    ranked = jnp.argsort(order).astype(jnp.int32)
    slot_ids = jnp.arange(total_slots, dtype=jnp.int32)
    in_owner = slot_ids // SLOTS == owner
    scores = jnp.where(in_owner, slot_ids - 4 * total_slots, ranked)
    scores = jnp.where((slot_ids == 0) & jnp.logical_not(in_owner), -3 * total_slots, scores)
    scores = jnp.where((slot_ids == total_slots - 1) & jnp.logical_not(in_owner), -2 * total_slots, scores)
    chosen = jnp.argsort(scores)[:NT].astype(jnp.int32)
    return jax.random.permutation(key_shuffle, chosen).astype(jnp.int32)


def block_levels(stream_key, dims, pieces, smallest, high):
    gain = 1.0
    for position, blocks in pieces:
        steps = jax.random.uniform(jax.random.fold_in(jax.random.fold_in(stream_key, 6), position), (blocks,), jnp.float32, smallest / len(pieces), high / len(pieces))
        gain = gain * jnp.repeat(jnp.exp(steps), dims[position] // blocks).reshape((-1,) + (1,) * (len(dims) - 1 - position))
    return gain


def normal_values(stream_key, extent, deviation, limit, cuts=(), held_as=jnp.bfloat16):
    array = deviation * jax.random.normal(stream_key, extent, jnp.float32)
    if cuts:
        array = array * block_levels(stream_key, extent, cuts, -0.22, 0.18)
    return jnp.clip(array, -limit, limit).astype(held_as)


def setup_inputs(seed: int = 0) -> dict:
    seeds = jax.random.split(jax.random.key(seed), 10)
    decoder_input = normal_values(seeds[0], (N_DP, C, NX, NY, NZ), 1.0, 6.0, ((0, 8), (2, 4)))
    cotangent = normal_values(seeds[1], (N_DP, C, NX, NY, NZ), 1.0, 6.0, ((0, 8), (2, 4)))
    encoder_input = normal_values(seeds[2], (N_DP, C, NX, NY, NZ), 1.0, 6.0, ((0, 8), (2, 4)))
    decoder_weights = normal_values(seeds[3], (2, 27, C * C), (27 * C) ** -0.5, 0.15625)
    other_grads = normal_values(seeds[4], (N_DP, N_SPACE, NT, 27, C * C), ((CX * NY * NZ) ** 0.5), 384.0, ((0, 8), (1, 4)))
    assignment = draw_assignment(jax.random.fold_in(seeds[9], 71), 0)
    moment_first = normal_values(seeds[6], (ALL_SLOTS, 27, C * C), 0.3, 4.0, ((0, 8), (2, 4)), jnp.float32)
    moment_second = jnp.clip(jnp.exp(math.log(2.0) - 4.6051702 * jax.random.uniform(seeds[7], (ALL_SLOTS, 27, C * C), jnp.float32) ** block_levels(seeds[7], (ALL_SLOTS, 27, C * C), ((0, 8), (2, 4)), -0.2, 0.2)), 0.02, 2.0)
    master_weights = normal_values(seeds[8], (ALL_SLOTS, 27, C * C), (27 * C) ** -0.5, 0.15625, ((0, 8), (2, 4)), jnp.float32)
    return {"decoder_input": decoder_input, "cotangent": cotangent, "encoder_input": encoder_input, "decoder_weights": decoder_weights, "other_grads": other_grads, "assignment": assignment, "moment_first": moment_first, "moment_second": moment_second, "master_weights": master_weights}


learn_rate = 0.002
decay_rate = 0.1
epsilon = 1e-08
bias_one = 1.0 - (0.9 ** 50) ** 2
bias_two = 1.0 - (0.999 ** 50) ** 2
tap_offsets = [(a, b, c) for a in (-1, 0, 1) for b in (-1, 0, 1) for c in (-1, 0, 1)]

def moved(field, shift_x, shift_y, shift_z):
    return jnp.roll(field, (-shift_x, -shift_y, -shift_z), axis=(1, 2, 3))

def forward_conv(field, kernel):
    result = jnp.zeros(field.shape, jnp.float32)
    for tap_number, (shift_x, shift_y, shift_z) in enumerate(tap_offsets):
        result = result + jnp.einsum('oi,ixyz->oxyz', kernel[tap_number].astype(jnp.float32), moved(field, shift_x, shift_y, shift_z).astype(jnp.float32))
    return result

def transposed_conv(grads, kernel):
    result = jnp.zeros(grads.shape, jnp.float32)
    for tap_number, (shift_x, shift_y, shift_z) in enumerate(tap_offsets):
        result = result + jnp.einsum('oi,oxyz->ixyz', kernel[tap_number].astype(jnp.float32), moved(grads, -shift_x, -shift_y, -shift_z).astype(jnp.float32))
    return result

def weight_grad(grads, field):
    parts = []
    for shift_x, shift_y, shift_z in tap_offsets:
        parts.append(jnp.einsum('oxyz,ixyz->oi', grads.astype(jnp.float32), moved(field, shift_x, shift_y, shift_z).astype(jnp.float32)))
    return jnp.stack(parts)

def reference(decoder_input, cotangent, encoder_input, decoder_weights, other_grads, assignment, moment_first, moment_second, master_weights):
    kernel_a = decoder_weights[0].reshape(27, C, C)
    kernel_b = decoder_weights[1].reshape(27, C, C)

    def per_box(items):
        dec_field, cot_field = items
        preact = forward_conv(dec_field, kernel_a)
        sigma = jax.nn.sigmoid(preact)
        hidden = (preact * sigma).astype(jnp.bfloat16)
        grad_b = weight_grad(cot_field, hidden)
        grad_hidden = transposed_conv(cot_field, kernel_b)
        grad_pre = (grad_hidden * sigma * (1.0 + preact * (1.0 - sigma))).astype(jnp.bfloat16)
        grad_a = weight_grad(grad_pre, dec_field)
        in_grad = transposed_conv(grad_pre, kernel_a).astype(jnp.bfloat16)
        return (in_grad, grad_a, grad_b)
    input_grad, grads_a, grads_b = lax.map(per_box, (decoder_input, cotangent))
    summed = lax.optimization_barrier(jnp.sum(other_grads, axis=(0, 1), dtype=jnp.float32))
    summed = summed.at[0].add(lax.optimization_barrier(jnp.sum(grads_a, axis=0)).reshape(27, C * C))
    summed = summed.at[1].add(lax.optimization_barrier(jnp.sum(grads_b, axis=0)).reshape(27, C * C))
    totals = summed / (N_DP * NX * NY * NZ) ** 0.5
    slot_grads = jnp.zeros((N_DP * SLOTS, 27, C * C), jnp.float32).at[assignment].set(totals)
    new_first = 0.9 * moment_first + 0.1 * slot_grads
    new_second = 0.999 * moment_second + 0.001 * slot_grads * slot_grads
    update = new_first / bias_one / (jnp.sqrt(new_second / bias_two) + epsilon)
    new_master = master_weights - learn_rate * (update + decay_rate * master_weights)
    new_params = new_master[assignment].astype(jnp.bfloat16)
    kernel_c = new_params[2].reshape(27, C, C)
    kernel_d = new_params[3].reshape(27, C, C)

    def encode(enc_field):
        first = forward_conv(enc_field, kernel_c)
        activ = (first * jax.nn.sigmoid(first)).astype(jnp.bfloat16)
        return (enc_field.astype(jnp.float32) + forward_conv(activ, kernel_d)).astype(jnp.bfloat16)
    encoder_out = lax.map(encode, encoder_input)
    return (input_grad, encoder_out, new_params, new_first, new_second, new_master)
```

```python
import functools
import math

import jax
import jax.numpy as jnp
from jax import lax
from jax.experimental import pallas as pl
from jax.experimental.pallas import tpu as pltpu
from jax.sharding import PartitionSpec as P

learn_rate = 0.002
decay_rate = 0.1
epsilon = 1e-08
bias_one = 1.0 - (0.9**50) ** 2
bias_two = 1.0 - (0.999**50) ** 2

TILE = 512
LANES = 128


def rolled(tile, shift):
    groups = tile.shape[1] // LANES
    return jnp.concatenate(
        [pltpu.roll(tile[:, g * LANES : (g + 1) * LANES], shift, 1) for g in range(groups)], axis=1
    )


def stack_planes(target, refs, rows):
    channels = refs[0].shape[2]
    for number, ref in enumerate(refs):
        for x in range(ref.shape[0]):
            plane = number * ref.shape[0] + x

            def row(y, _, ref=ref, x=x, plane=plane):
                value = ref[x, y]
                for b in range(3):
                    at = plane * rows + lax.rem(y + 1 - b + rows, rows)
                    at = pl.multiple_of(at * LANES, LANES)
                    target[b * channels : (b + 1) * channels, pl.ds(at, LANES)] = value
                return 0

            lax.fori_loop(0, rows, row, 0)


def stack_tile(target, tile, n, rows):
    channels = tile.shape[0]
    per = tile.shape[1] // LANES
    for g in range(per):
        r = n * per + g
        plane, y = r // rows, lax.rem(r, rows)
        for b in range(3):
            at = plane * rows + lax.rem(y + 1 - b + rows, rows)
            at = pl.multiple_of(at * LANES, LANES)
            target[b * channels : (b + 1) * channels, pl.ds(at, LANES)] = tile[
                :, g * LANES : (g + 1) * LANES
            ]


def conv_tile(weights, stacked, n, cells, first_plane=0):
    channels = weights.shape[1] // 3
    total = None
    for a in range(3):
        at = pl.multiple_of(n * TILE + (a + first_plane) * cells, TILE)
        part = jnp.dot(
            weights[a], stacked[:, pl.ds(at, TILE)], preferred_element_type=jnp.float32
        )
        total = part if total is None else total + part
    return (
        total[channels : 2 * channels]
        + rolled(total[:channels], 1)
        + rolled(total[2 * channels :], LANES - 1)
    )


def store_rows(out_ref, tile, n, rows):
    per = tile.shape[1] // LANES
    for g in range(per):
        r = n * per + g
        out_ref[r // rows, lax.rem(r, rows)] = tile[:, g * LANES : (g + 1) * LANES]


def shifted_stack(target, n, tile):
    channels = tile.shape[0]
    at = pl.ds(pl.multiple_of(n * TILE, TILE), TILE)
    wide = tile.astype(jnp.float32)
    target[:channels, at] = rolled(wide, LANES - 1).astype(jnp.bfloat16)
    target[channels : 2 * channels, at] = tile
    target[2 * channels :, at] = rolled(wide, 1).astype(jnp.bfloat16)


def decoder_kernel(
    rows,
    dec_low, dec_mid, dec_high, cot_low, cot_mid, cot_high, w_a, w_bt, w_at,
    out_grad, out_a, out_b,
    f_dec, f_cot, f_hid, f_pre, s_cot, s_pre,
):
    thick = dec_mid.shape[0]
    cells = rows * LANES
    channels = dec_mid.shape[2]
    stack_planes(f_dec, (dec_low, dec_mid, dec_high), rows)
    stack_planes(f_cot, (cot_low, cot_mid, cot_high), rows)
    skip = thick - 1
    per_plane = cells // TILE

    def first(n, _):
        preact = conv_tile(w_a, f_dec, n, cells, skip - 1)
        grad_hidden = conv_tile(w_bt, f_cot, n, cells, skip - 1)
        sigma = jax.nn.sigmoid(preact)
        stack_tile(f_hid, (preact * sigma).astype(jnp.bfloat16), n, rows)
        grad_pre = grad_hidden * sigma * (1.0 + preact * (1.0 - sigma))
        stack_tile(f_pre, grad_pre.astype(jnp.bfloat16), n, rows)
        return 0

    lax.fori_loop(0, (thick + 2) * per_plane, first, 0)
    out_a[...] = jnp.zeros_like(out_a)
    out_b[...] = jnp.zeros_like(out_b)
    nt = (((1,), (1,)), ((), ()))

    def second(n, _):
        at = pl.ds(pl.multiple_of(n * TILE + cells, TILE), TILE)
        shifted_stack(s_pre, n, f_pre[channels : 2 * channels, at])
        at = pl.ds(pl.multiple_of(n * TILE + thick * cells, TILE), TILE)
        shifted_stack(s_cot, n, f_cot[channels : 2 * channels, at])
        here = pl.ds(pl.multiple_of(n * TILE, TILE), TILE)
        for a in range(3):
            at = pl.ds(pl.multiple_of(n * TILE + a * cells, TILE), TILE)
            out_b[a] += lax.dot_general(
                s_cot[:, here], f_hid[:, at], nt, preferred_element_type=jnp.float32
            )
            at = pl.ds(pl.multiple_of(n * TILE + (a + thick - 1) * cells, TILE), TILE)
            out_a[a] += lax.dot_general(
                s_pre[:, here], f_dec[:, at], nt, preferred_element_type=jnp.float32
            )
        tile = conv_tile(w_at, f_pre, n, cells)
        store_rows(out_grad, tile.astype(jnp.bfloat16), n, rows)
        return 0

    lax.fori_loop(0, thick * per_plane, second, 0)


def encoder_kernel(rows, low, mid, high, w_c, w_d, out, f_enc, f_act):
    thick = mid.shape[0]
    cells = rows * LANES
    channels = mid.shape[2]
    stack_planes(f_enc, (low, mid, high), rows)
    skip = thick - 1
    per_plane = cells // TILE

    def first(n, _):
        value = conv_tile(w_c, f_enc, n, cells, skip - 1)
        stack_tile(f_act, (value * jax.nn.sigmoid(value)).astype(jnp.bfloat16), n, rows)
        return 0

    lax.fori_loop(0, (thick + 2) * per_plane, first, 0)

    def second(n, _):
        value = conv_tile(w_d, f_act, n, cells)
        at = pl.ds(pl.multiple_of(n * TILE + thick * cells, TILE), TILE)
        base = f_enc[channels : 2 * channels, at].astype(jnp.float32)
        store_rows(out, (base + value).astype(jnp.bfloat16), n, rows)
        return 0

    lax.fori_loop(0, thick * per_plane, second, 0)


def whole(count):
    return [pl.BlockSpec(memory_space=pltpu.VMEM)] * count


def stacked_weights(kernel, channels):
    taps = kernel.reshape(3, 3, 3, channels, channels)
    return taps.transpose(0, 2, 3, 1, 4).reshape(3, 3 * channels, 3 * channels)


def turned_weights(kernel, channels):
    taps = kernel.reshape(3, 3, 3, channels, channels)[::-1, ::-1, ::-1]
    return taps.transpose(0, 2, 4, 1, 3).reshape(3, 3 * channels, 3 * channels)


def unstacked(grad, channels):
    taps = grad.reshape(3, 3, channels, 3, channels).transpose(0, 3, 1, 2, 4)
    return taps.reshape(27, channels * channels)


def neighbours(field):
    count = lax.axis_size("space")
    forward = [(i, (i + 1) % count) for i in range(count)]
    backward = [(target, source) for source, target in forward]
    low = lax.ppermute(field, "space", forward)
    high = lax.ppermute(field, "space", backward)
    return low, field, high


def adamw(moment_first, moment_second, master_weights, grads):
    new_first = 0.9 * moment_first + 0.1 * grads
    new_second = 0.999 * moment_second + 0.001 * grads * grads
    update = new_first / bias_one / (jnp.sqrt(new_second / bias_two) + epsilon)
    new_master = master_weights - learn_rate * (update + decay_rate * master_weights)
    return new_first, new_second, new_master


def per_device(
    decoder_input,
    cotangent,
    encoder_input,
    decoder_weights,
    other_grads,
    assignment,
    moment_first,
    moment_second,
    master_weights,
):
    channels, thick, rows, lanes = decoder_input.shape[1:]
    replicas = lax.axis_size("dp")
    slabs = lax.axis_size("space")
    slots, taps, share = moment_first.shape
    tensors = assignment.shape[0]
    every_slot = replicas * slots
    cells = rows * lanes
    scale = 1.0 / math.sqrt(replicas * thick * slabs * cells)
    params = pltpu.CompilerParams(vmem_limit_bytes=48 * 1024 * 1024)

    match = assignment[None, :] == jnp.arange(every_slot, dtype=jnp.int32)[:, None]
    used = jnp.any(match, axis=1)
    tensor_of = jnp.argmax(match, axis=1).astype(jnp.int32)
    by_slot = jnp.where(
        used[:, None, None], jnp.take(other_grads[0, 0], tensor_of, axis=0), 0
    ).astype(jnp.bfloat16)
    owned = lax.psum_scatter(by_slot, "dp", scatter_dimension=0, tiled=True)
    owned = lax.psum_scatter(owned, "space", scatter_dimension=2, tiled=True)
    owned = owned.astype(jnp.float32)

    dec = neighbours(decoder_input[0].transpose(1, 2, 0, 3))
    cot = neighbours(cotangent[0].transpose(1, 2, 0, 3))
    w_a = stacked_weights(decoder_weights[0], channels)
    w_at = turned_weights(decoder_weights[0], channels)
    w_bt = turned_weights(decoder_weights[1], channels)
    wide = 3 * channels
    field = jax.ShapeDtypeStruct((thick, rows, channels, lanes), jnp.bfloat16)
    small = jax.ShapeDtypeStruct((3, wide, wide), jnp.float32)
    bf = jnp.bfloat16
    conv_flops = 2 * 27 * channels * channels * cells
    input_grad, grad_a, grad_b = pl.pallas_call(
        functools.partial(decoder_kernel, rows),
        out_shape=(field, small, small),
        in_specs=whole(9),
        out_specs=tuple(whole(3)),
        scratch_shapes=[
            pltpu.VMEM((wide, 3 * thick * cells), bf),
            pltpu.VMEM((wide, 3 * thick * cells), bf),
            pltpu.VMEM((wide, (thick + 2) * cells), bf),
            pltpu.VMEM((wide, (thick + 2) * cells), bf),
            pltpu.VMEM((wide, thick * cells), bf),
            pltpu.VMEM((wide, thick * cells), bf),
        ],
        compiler_params=params,
        cost_estimate=pl.CostEstimate(
            flops=30 * conv_flops, bytes_accessed=8 * 2**20, transcendentals=0
        ),
        name="decoder",
    )(*dec, *cot, w_a, w_bt, w_at)
    input_grad = input_grad.transpose(2, 0, 1, 3)[None]

    pair = jnp.stack([unstacked(grad_a, channels), unstacked(grad_b, channels)])
    pair = lax.psum_scatter(pair.astype(bf), "space", scatter_dimension=2, tiled=True)
    pair = lax.psum(pair, "dp").astype(jnp.float32)

    mine = lax.axis_index("dp") * slots + jnp.arange(slots, dtype=jnp.int32)
    early = adamw(moment_first, moment_second, master_weights, owned * scale)[2]
    gathered = lax.all_gather(early.astype(bf), ("dp", "space"), axis=0)
    gathered = gathered.reshape(replicas, slabs, slots, taps, share)
    picked = gathered[assignment // slots, :, lax.rem(assignment, slots)]

    is_a = (mine == assignment[0])[:, None, None]
    is_b = (mine == assignment[1])[:, None, None]
    owned = owned + jnp.where(is_a, pair[0], 0.0) + jnp.where(is_b, pair[1], 0.0)
    new_first, new_second, new_master = adamw(
        moment_first, moment_second, master_weights, owned * scale
    )
    rounded = new_master.astype(bf)
    late = jnp.stack(
        [
            jnp.sum(jnp.where(is_a, rounded, 0), axis=0),
            jnp.sum(jnp.where(is_b, rounded, 0), axis=0),
        ]
    ).astype(bf)
    late = lax.psum(late, "dp")
    late = lax.all_gather(late, "space", axis=2, tiled=True)
    rest = picked[2:].transpose(0, 2, 1, 3).reshape(tensors - 2, taps, slabs * share)
    new_params = jnp.concatenate([late, rest], axis=0)

    enc = neighbours(encoder_input[0].transpose(1, 2, 0, 3))
    w_c = stacked_weights(rest[0], channels)
    w_d = stacked_weights(rest[1], channels)
    encoder_out = pl.pallas_call(
        functools.partial(encoder_kernel, rows),
        out_shape=field,
        in_specs=whole(5),
        out_specs=whole(1)[0],
        scratch_shapes=[
            pltpu.VMEM((wide, 3 * thick * cells), bf),
            pltpu.VMEM((wide, (thick + 2) * cells), bf),
        ],
        compiler_params=params,
        cost_estimate=pl.CostEstimate(
            flops=12 * conv_flops, bytes_accessed=4 * 2**20, transcendentals=0
        ),
        name="encoder",
    )(*enc, w_c, w_d)
    encoder_out = encoder_out.transpose(2, 0, 1, 3)[None]
    return (input_grad, encoder_out, new_params, new_first, new_second, new_master)


def solution(mesh):
    in_specs = (
        P("dp", None, "space", None, None),
        P("dp", None, "space", None, None),
        P("dp", None, "space", None, None),
        P(),
        P("dp", "space", None, None, None),
        P(),
        P("dp", None, "space"),
        P("dp", None, "space"),
        P("dp", None, "space"),
    )
    out_specs = (
        P("dp", None, "space", None, None),
        P("dp", None, "space", None, None),
        P(),
        P("dp", None, "space"),
        P("dp", None, "space"),
        P("dp", None, "space"),
    )
    return jax.shard_map(
        per_device, mesh=mesh, in_specs=in_specs, out_specs=out_specs, check_vma=False
    )
```

```python
import functools
import math

import jax
import jax.numpy as jnp
from jax import lax
from jax.experimental import pallas as pl
from jax.experimental.pallas import tpu as pltpu
from jax.sharding import PartitionSpec as P

learn_rate = 0.002
decay_rate = 0.1
epsilon = 1e-08
bias_one = 1.0 - (0.9**50) ** 2
bias_two = 1.0 - (0.999**50) ** 2

TILE = 512
LANES = 128


def rolled(tile, shift):
    groups = tile.shape[1] // LANES
    return jnp.concatenate(
        [pltpu.roll(tile[:, g * LANES : (g + 1) * LANES], shift, 1) for g in range(groups)], axis=1
    )


def stack_planes(target, refs, rows):
    channels = refs[0].shape[2]
    for number, ref in enumerate(refs):
        for x in range(ref.shape[0]):
            plane = number * ref.shape[0] + x

            def row(y, _, ref=ref, x=x, plane=plane):
                value = ref[x, y]
                for b in range(3):
                    at = plane * rows + lax.rem(y + 1 - b + rows, rows)
                    at = pl.multiple_of(at * LANES, LANES)
                    target[b * channels : (b + 1) * channels, pl.ds(at, LANES)] = value
                return 0

            lax.fori_loop(0, rows, row, 0)


def stack_tile(target, tile, n, rows):
    channels = tile.shape[0]
    per = tile.shape[1] // LANES
    for g in range(per):
        r = n * per + g
        plane, y = r // rows, lax.rem(r, rows)
        for b in range(3):
            at = plane * rows + lax.rem(y + 1 - b + rows, rows)
            at = pl.multiple_of(at * LANES, LANES)
            target[b * channels : (b + 1) * channels, pl.ds(at, LANES)] = tile[
                :, g * LANES : (g + 1) * LANES
            ]


def conv_tile(weights, stacked, n, cells, first_plane=0):
    channels = weights.shape[1] // 3
    total = None
    for a in range(3):
        at = pl.multiple_of(n * TILE + (a + first_plane) * cells, TILE)
        part = jnp.dot(
            weights[a], stacked[:, pl.ds(at, TILE)], preferred_element_type=jnp.float32
        )
        total = part if total is None else total + part
    return (
        total[channels : 2 * channels]
        + rolled(total[:channels], 1)
        + rolled(total[2 * channels :], LANES - 1)
    )


def store_rows(out_ref, tile, n, rows):
    per = tile.shape[1] // LANES
    for g in range(per):
        r = n * per + g
        out_ref[r // rows, lax.rem(r, rows)] = tile[:, g * LANES : (g + 1) * LANES]


def shifted_stack(target, n, tile):
    channels = tile.shape[0]
    at = pl.ds(pl.multiple_of(n * TILE, TILE), TILE)
    wide = tile.astype(jnp.float32)
    target[:channels, at] = rolled(wide, LANES - 1).astype(jnp.bfloat16)
    target[channels : 2 * channels, at] = tile
    target[2 * channels :, at] = rolled(wide, 1).astype(jnp.bfloat16)


def decoder_kernel(
    rows,
    dec_low, dec_mid, dec_high, cot_low, cot_mid, cot_high, w_a, w_bt, w_at,
    out_grad, out_a, out_b,
    f_dec, f_cot, f_hid, f_pre, s_cot, s_pre,
):
    thick = dec_mid.shape[0]
    cells = rows * LANES
    channels = dec_mid.shape[2]
    stack_planes(f_dec, (dec_low, dec_mid, dec_high), rows)
    stack_planes(f_cot, (cot_low, cot_mid, cot_high), rows)
    skip = thick - 1
    per_plane = cells // TILE

    def first(n, _):
        preact = conv_tile(w_a, f_dec, n, cells, skip - 1)
        grad_hidden = conv_tile(w_bt, f_cot, n, cells, skip - 1)
        sigma = jax.nn.sigmoid(preact)
        stack_tile(f_hid, (preact * sigma).astype(jnp.bfloat16), n, rows)
        grad_pre = grad_hidden * sigma * (1.0 + preact * (1.0 - sigma))
        stack_tile(f_pre, grad_pre.astype(jnp.bfloat16), n, rows)
        return 0

    lax.fori_loop(0, (thick + 2) * per_plane, first, 0)
    out_a[...] = jnp.zeros_like(out_a)
    out_b[...] = jnp.zeros_like(out_b)
    nt = (((1,), (1,)), ((), ()))

    def second(n, _):
        at = pl.ds(pl.multiple_of(n * TILE + cells, TILE), TILE)
        shifted_stack(s_pre, n, f_pre[channels : 2 * channels, at])
        at = pl.ds(pl.multiple_of(n * TILE + thick * cells, TILE), TILE)
        shifted_stack(s_cot, n, f_cot[channels : 2 * channels, at])
        here = pl.ds(pl.multiple_of(n * TILE, TILE), TILE)
        for a in range(3):
            at = pl.ds(pl.multiple_of(n * TILE + a * cells, TILE), TILE)
            out_b[a] += lax.dot_general(
                s_cot[:, here], f_hid[:, at], nt, preferred_element_type=jnp.float32
            )
            at = pl.ds(pl.multiple_of(n * TILE + (a + thick - 1) * cells, TILE), TILE)
            out_a[a] += lax.dot_general(
                s_pre[:, here], f_dec[:, at], nt, preferred_element_type=jnp.float32
            )
        tile = conv_tile(w_at, f_pre, n, cells)
        store_rows(out_grad, tile.astype(jnp.bfloat16), n, rows)
        return 0

    lax.fori_loop(0, thick * per_plane, second, 0)


def encoder_kernel(rows, low, mid, high, w_c, w_d, out, f_enc, f_act):
    thick = mid.shape[0]
    cells = rows * LANES
    channels = mid.shape[2]
    stack_planes(f_enc, (low, mid, high), rows)
    skip = thick - 1
    per_plane = cells // TILE

    def first(n, _):
        value = conv_tile(w_c, f_enc, n, cells, skip - 1)
        stack_tile(f_act, (value * jax.nn.sigmoid(value)).astype(jnp.bfloat16), n, rows)
        return 0

    lax.fori_loop(0, (thick + 2) * per_plane, first, 0)

    def second(n, _):
        value = conv_tile(w_d, f_act, n, cells)
        at = pl.ds(pl.multiple_of(n * TILE + thick * cells, TILE), TILE)
        base = f_enc[channels : 2 * channels, at].astype(jnp.float32)
        store_rows(out, (base + value).astype(jnp.bfloat16), n, rows)
        return 0

    lax.fori_loop(0, thick * per_plane, second, 0)


def flipped(index, bit):
    return index + (1 << bit) * (1 - 2 * lax.rem(index // (1 << bit), 2))


def crossed(left, right, bits):
    total = 0
    for bit in range(bits):
        one = lax.rem(left // (1 << bit), 2)
        two = lax.rem(right // (1 << bit), 2)
        total = total + (1 << bit) * (one + two - 2 * one * two)
    return total


def subset(bits):
    sums = [0]
    for bit in bits:
        sums = sums + [one + bit for one in sums]
    return sums


def owner_kernel(
    replicas, slabs, scale,
    tensor_of, used, assignment, grads, first, second, master,
    params, out_first, out_second, out_master,
    work, landed, held, send_one, recv_one, send_two, recv_two,
):
    slots, taps, share = first.shape
    me, lane = lax.axis_index("dp"), lax.axis_index("space")
    dp_bits, space_bits = replicas.bit_length() - 1, slabs.bit_length() - 1
    core = lax.rem(me, 2)
    turn = [(k, (k + 1) % space_bits) for k in range(space_bits)]
    weight = [(1 - core) * (1 << one) + core * (1 << two) for one, two in turn]
    by_core = (flipped(me, 0), lane)
    by_space = [
        (me, (1 - core) * flipped(lane, one) + core * flipped(lane, two)) for one, two in turn
    ]
    by_dp = [(flipped(me, bit), lane) for bit in range(1, dp_bits)]

    barrier = pltpu.get_barrier_semaphore()
    for partner in [by_core] + by_space + by_dp:
        pl.semaphore_signal(
            barrier, inc=1, device_id=partner, device_id_type=pl.DeviceIdType.MESH
        )
    pl.semaphore_wait(barrier, dp_bits + space_bits)

    def build(odd):
        def one(n, _):
            apart = 2 * (n // slabs) + odd
            aside = lax.rem(n, slabs)
            owner = crossed(me, apart, dp_bits)
            column = crossed(lane, aside, space_bits)
            columns = pl.ds(pl.multiple_of(column * share, share), share)
            for slot in range(slots):
                number = owner * slots + slot
                value = grads[tensor_of[number], :, columns].astype(jnp.float32)
                work[apart * slabs + aside, slot] = (value * used[number]).astype(jnp.bfloat16)
            return 0

        lax.fori_loop(0, replicas * slabs // 2, one, 0)

    steps = [
        (
            by_core,
            [
                ((rd + 1) * slabs + rs, rd * slabs + rs)
                for rd in range(0, replicas, 2)
                for rs in range(slabs)
            ],
        )
    ]
    for k in range(space_bits):
        later = subset(weight[k + 1 :][::-1])[::-1]
        pairs = [
            (rd * slabs + rs + weight[k], rd * slabs + rs)
            for rs in later
            for rd in range(0, replicas, 2)
        ]
        steps.append((by_space[k], pairs))
    for bit in range(1, dp_bits):
        later = subset([1 << j for j in range(bit + 1, dp_bits)][::-1])[::-1]
        pairs = [((rd + (1 << bit)) * slabs, rd * slabs) for rd in later]
        steps.append((by_dp[bit - 1], pairs))

    count = 0
    pending, sent = [], []
    for number, (partner, pairs) in enumerate(steps):
        if number == 0:
            build(1)
        copies = []
        for source, target in pairs:
            copy = pltpu.make_async_remote_copy(
                src_ref=work.at[source],
                dst_ref=landed.at[count],
                send_sem=send_one.at[count],
                recv_sem=recv_one.at[count],
                device_id=partner,
                device_id_type=pl.DeviceIdType.MESH,
            )
            copy.start()
            copies.append((copy, target, count))
            count += 1
        if number == 0:
            build(0)
        for copy, target, at in copies:
            copy.wait_recv()
            total = work[target].astype(jnp.float32) + landed[at].astype(jnp.float32)
            work[target] = total.astype(jnp.bfloat16)
            sent.append(copy)
    for copy in sent:
        copy.wait_send()

    owned = work[0].astype(jnp.float32) * scale
    new_first = 0.9 * first[...] + 0.1 * owned
    new_second = 0.999 * second[...] + 0.001 * owned * owned
    update = new_first / bias_one / (jnp.sqrt(new_second / bias_two) + epsilon)
    new_master = master[...] - learn_rate * (update + decay_rate * master[...])
    out_first[...] = new_first
    out_second[...] = new_second
    out_master[...] = new_master
    held[0] = new_master.astype(jnp.bfloat16)

    count = 0
    have = [0]
    sent = []
    moves = [(by_dp[bit - 1], (1 << bit) * slabs) for bit in range(dp_bits - 1, 0, -1)]
    moves += [(by_space[k], weight[k]) for k in range(space_bits - 1, -1, -1)]
    moves.append((by_core, slabs))
    for number, (partner, gap) in enumerate(moves):
        if number == len(moves) - 1:
            have = [rd * slabs + rs for rd in range(0, replicas, 2) for rs in range(slabs)]
        copies = []
        for source in have:
            copy = pltpu.make_async_remote_copy(
                src_ref=held.at[source],
                dst_ref=held.at[source + gap],
                send_sem=send_two.at[count],
                recv_sem=recv_two.at[count],
                device_id=partner,
                device_id_type=pl.DeviceIdType.MESH,
            )
            copy.start()
            copies.append(copy)
            count += 1
        for copy in copies:
            copy.wait_recv()
        sent += copies
        have = have + [one + gap for one in have]
    for copy in sent:
        copy.wait_send()

    for column in range(slabs):
        aside = crossed(lane, column, space_bits)

        def place(tensor, _, column=column, aside=aside):
            slot = assignment[tensor]
            apart = crossed(me, slot // slots, dp_bits)
            params[tensor, :, column * share : (column + 1) * share] = held[
                apart * slabs + aside, lax.rem(slot, slots)
            ]
            return 0

        lax.fori_loop(0, params.shape[0], place, 0)


def whole(count):
    return [pl.BlockSpec(memory_space=pltpu.VMEM)] * count


def stacked_weights(kernel, channels):
    taps = kernel.reshape(3, 3, 3, channels, channels)
    return taps.transpose(0, 2, 3, 1, 4).reshape(3, 3 * channels, 3 * channels)


def turned_weights(kernel, channels):
    taps = kernel.reshape(3, 3, 3, channels, channels)[::-1, ::-1, ::-1]
    return taps.transpose(0, 2, 4, 1, 3).reshape(3, 3 * channels, 3 * channels)


def unstacked(grad, channels):
    taps = grad.reshape(3, 3, channels, 3, channels).transpose(0, 3, 1, 2, 4)
    return taps.reshape(27, channels * channels)


def neighbours(field):
    count = lax.axis_size("space")
    forward = [(i, (i + 1) % count) for i in range(count)]
    backward = [(target, source) for source, target in forward]
    low = lax.ppermute(field, "space", forward)
    high = lax.ppermute(field, "space", backward)
    return low, field, high


def per_device(
    decoder_input,
    cotangent,
    encoder_input,
    decoder_weights,
    other_grads,
    assignment,
    moment_first,
    moment_second,
    master_weights,
):
    channels, thick, rows, lanes = decoder_input.shape[1:]
    replicas = lax.axis_size("dp")
    slabs = lax.axis_size("space")
    slots, taps, share = moment_first.shape
    tensors = assignment.shape[0]
    every_slot = replicas * slots
    cells = rows * lanes
    scale = 1.0 / math.sqrt(replicas * thick * slabs * cells)
    params = pltpu.CompilerParams(vmem_limit_bytes=48 * 1024 * 1024)

    dec = neighbours(decoder_input[0].transpose(1, 2, 0, 3))
    cot = neighbours(cotangent[0].transpose(1, 2, 0, 3))
    w_a = stacked_weights(decoder_weights[0], channels)
    w_at = turned_weights(decoder_weights[0], channels)
    w_bt = turned_weights(decoder_weights[1], channels)
    wide = 3 * channels
    field = jax.ShapeDtypeStruct((thick, rows, channels, lanes), jnp.bfloat16)
    small = jax.ShapeDtypeStruct((3, wide, wide), jnp.float32)
    bf = jnp.bfloat16
    conv_flops = 2 * 27 * channels * channels * cells
    input_grad, grad_a, grad_b = pl.pallas_call(
        functools.partial(decoder_kernel, rows),
        out_shape=(field, small, small),
        in_specs=whole(9),
        out_specs=tuple(whole(3)),
        scratch_shapes=[
            pltpu.VMEM((wide, 3 * thick * cells), bf),
            pltpu.VMEM((wide, 3 * thick * cells), bf),
            pltpu.VMEM((wide, (thick + 2) * cells), bf),
            pltpu.VMEM((wide, (thick + 2) * cells), bf),
            pltpu.VMEM((wide, thick * cells), bf),
            pltpu.VMEM((wide, thick * cells), bf),
        ],
        compiler_params=params,
        cost_estimate=pl.CostEstimate(
            flops=30 * conv_flops, bytes_accessed=8 * 2**20, transcendentals=0
        ),
        name="decoder",
    )(*dec, *cot, w_a, w_bt, w_at)
    input_grad = input_grad.transpose(2, 0, 1, 3)[None]

    pair = jnp.stack([unstacked(grad_a, channels), unstacked(grad_b, channels)])
    match = assignment[None, :] == jnp.arange(every_slot, dtype=jnp.int32)[:, None]
    used = jnp.any(match, axis=1).astype(jnp.float32)
    tensor_of = jnp.argmax(match, axis=1).astype(jnp.int32)
    mixed = (other_grads[0, 0, :2].astype(jnp.float32) + pair).astype(bf)
    grads = jnp.concatenate([mixed, other_grads[0, 0, 2:]], axis=0)
    chunks = replicas * slabs
    state = jax.ShapeDtypeStruct(moment_first.shape, jnp.float32)
    scalars = [pl.BlockSpec(memory_space=pltpu.SMEM)] * 3
    new_params, new_first, new_second, new_master = pl.pallas_call(
        functools.partial(owner_kernel, replicas, slabs, scale),
        out_shape=(
            jax.ShapeDtypeStruct((tensors, taps, slabs * share), bf),
            state,
            state,
            state,
        ),
        in_specs=scalars + whole(4),
        out_specs=tuple(whole(4)),
        scratch_shapes=[
            pltpu.VMEM((chunks, slots, taps, share), bf),
            pltpu.VMEM((chunks - 1, slots, taps, share), bf),
            pltpu.VMEM((chunks, slots, taps, share), bf),
        ]
        + [pltpu.SemaphoreType.DMA((chunks - 1,))] * 4,
        compiler_params=pltpu.CompilerParams(
            vmem_limit_bytes=56 * 1024 * 1024, collective_id=0, has_side_effects=True
        ),
        cost_estimate=pl.CostEstimate(
            flops=2**24, bytes_accessed=16 * 2**20, transcendentals=0
        ),
        name="owners",
    )(tensor_of, used, assignment, grads, moment_first, moment_second, master_weights)
    rest = new_params[2:4]

    enc = neighbours(encoder_input[0].transpose(1, 2, 0, 3))
    w_c = stacked_weights(rest[0], channels)
    w_d = stacked_weights(rest[1], channels)
    encoder_out = pl.pallas_call(
        functools.partial(encoder_kernel, rows),
        out_shape=field,
        in_specs=whole(5),
        out_specs=whole(1)[0],
        scratch_shapes=[
            pltpu.VMEM((wide, 3 * thick * cells), bf),
            pltpu.VMEM((wide, (thick + 2) * cells), bf),
        ],
        compiler_params=params,
        cost_estimate=pl.CostEstimate(
            flops=12 * conv_flops, bytes_accessed=4 * 2**20, transcendentals=0
        ),
        name="encoder",
    )(*enc, w_c, w_d)
    encoder_out = encoder_out.transpose(2, 0, 1, 3)[None]
    return (input_grad, encoder_out, new_params, new_first, new_second, new_master)


def solution(mesh):
    in_specs = (
        P("dp", None, "space", None, None),
        P("dp", None, "space", None, None),
        P("dp", None, "space", None, None),
        P(),
        P("dp", "space", None, None, None),
        P(),
        P("dp", None, "space"),
        P("dp", None, "space"),
        P("dp", None, "space"),
    )
    out_specs = (
        P("dp", None, "space", None, None),
        P("dp", None, "space", None, None),
        P(),
        P("dp", None, "space"),
        P("dp", None, "space"),
        P("dp", None, "space"),
    )
    return jax.shard_map(
        per_device, mesh=mesh, in_specs=in_specs, out_specs=out_specs, check_vma=False
    )
```

```python
import functools
import math

import jax
import jax.numpy as jnp
from jax import lax
from jax.experimental import pallas as pl
from jax.experimental.pallas import tpu as pltpu
from jax.sharding import PartitionSpec as P

learn_rate = 0.002
decay_rate = 0.1
epsilon = 1e-08
bias_one = 1.0 - (0.9**50) ** 2
bias_two = 1.0 - (0.999**50) ** 2

TILE = 512
LANES = 128


def rolled(tile, shift):
    groups = tile.shape[1] // LANES
    return jnp.concatenate(
        [pltpu.roll(tile[:, g * LANES : (g + 1) * LANES], shift, 1) for g in range(groups)], axis=1
    )


def stack_planes(target, refs, rows):
    channels = refs[0].shape[2]
    for number, ref in enumerate(refs):
        for x in range(ref.shape[0]):
            plane = number * ref.shape[0] + x

            def row(y, _, ref=ref, x=x, plane=plane):
                value = ref[x, y]
                for b in range(3):
                    at = plane * rows + lax.rem(y + 1 - b + rows, rows)
                    at = pl.multiple_of(at * LANES, LANES)
                    target[b * channels : (b + 1) * channels, pl.ds(at, LANES)] = value
                return 0

            lax.fori_loop(0, rows, row, 0)


def stack_tile(target, tile, n, rows):
    channels = tile.shape[0]
    per = tile.shape[1] // LANES
    for g in range(per):
        r = n * per + g
        plane, y = r // rows, lax.rem(r, rows)
        for b in range(3):
            at = plane * rows + lax.rem(y + 1 - b + rows, rows)
            at = pl.multiple_of(at * LANES, LANES)
            target[b * channels : (b + 1) * channels, pl.ds(at, LANES)] = tile[
                :, g * LANES : (g + 1) * LANES
            ]


def conv_tile(weights, stacked, n, cells, first_plane=0):
    channels = weights.shape[1] // 3
    total = None
    for a in range(3):
        at = pl.multiple_of(n * TILE + (a + first_plane) * cells, TILE)
        part = jnp.dot(
            weights[a], stacked[:, pl.ds(at, TILE)], preferred_element_type=jnp.float32
        )
        total = part if total is None else total + part
    return (
        total[channels : 2 * channels]
        + rolled(total[:channels], 1)
        + rolled(total[2 * channels :], LANES - 1)
    )


def store_rows(out_ref, tile, n, rows):
    per = tile.shape[1] // LANES
    for g in range(per):
        r = n * per + g
        out_ref[r // rows, lax.rem(r, rows)] = tile[:, g * LANES : (g + 1) * LANES]


def shifted_stack(target, n, tile):
    channels = tile.shape[0]
    at = pl.ds(pl.multiple_of(n * TILE, TILE), TILE)
    wide = tile.astype(jnp.float32)
    target[:channels, at] = rolled(wide, LANES - 1).astype(jnp.bfloat16)
    target[channels : 2 * channels, at] = tile
    target[2 * channels :, at] = rolled(wide, 1).astype(jnp.bfloat16)


def decoder_kernel(
    rows,
    dec_low, dec_mid, dec_high, cot_low, cot_mid, cot_high, w_a, w_bt, w_at,
    out_grad, out_a, out_b,
    f_dec, f_cot, f_hid, f_pre, s_cot, s_pre,
):
    thick = dec_mid.shape[0]
    cells = rows * LANES
    channels = dec_mid.shape[2]
    stack_planes(f_dec, (dec_low, dec_mid, dec_high), rows)
    stack_planes(f_cot, (cot_low, cot_mid, cot_high), rows)
    skip = thick - 1
    per_plane = cells // TILE

    def first(n, _):
        preact = conv_tile(w_a, f_dec, n, cells, skip - 1)
        grad_hidden = conv_tile(w_bt, f_cot, n, cells, skip - 1)
        sigma = jax.nn.sigmoid(preact)
        stack_tile(f_hid, (preact * sigma).astype(jnp.bfloat16), n, rows)
        grad_pre = grad_hidden * sigma * (1.0 + preact * (1.0 - sigma))
        stack_tile(f_pre, grad_pre.astype(jnp.bfloat16), n, rows)
        return 0

    lax.fori_loop(0, (thick + 2) * per_plane, first, 0)
    out_a[...] = jnp.zeros_like(out_a)
    out_b[...] = jnp.zeros_like(out_b)
    nt = (((1,), (1,)), ((), ()))

    def second(n, _):
        at = pl.ds(pl.multiple_of(n * TILE + cells, TILE), TILE)
        shifted_stack(s_pre, n, f_pre[channels : 2 * channels, at])
        at = pl.ds(pl.multiple_of(n * TILE + thick * cells, TILE), TILE)
        shifted_stack(s_cot, n, f_cot[channels : 2 * channels, at])
        here = pl.ds(pl.multiple_of(n * TILE, TILE), TILE)
        for a in range(3):
            at = pl.ds(pl.multiple_of(n * TILE + a * cells, TILE), TILE)
            out_b[a] += lax.dot_general(
                s_cot[:, here], f_hid[:, at], nt, preferred_element_type=jnp.float32
            )
            at = pl.ds(pl.multiple_of(n * TILE + (a + thick - 1) * cells, TILE), TILE)
            out_a[a] += lax.dot_general(
                s_pre[:, here], f_dec[:, at], nt, preferred_element_type=jnp.float32
            )
        tile = conv_tile(w_at, f_pre, n, cells)
        store_rows(out_grad, tile.astype(jnp.bfloat16), n, rows)
        return 0

    lax.fori_loop(0, thick * per_plane, second, 0)


def encoder_kernel(rows, low, mid, high, w_c, w_d, out, f_enc, f_act):
    thick = mid.shape[0]
    cells = rows * LANES
    channels = mid.shape[2]
    stack_planes(f_enc, (low, mid, high), rows)
    skip = thick - 1
    per_plane = cells // TILE

    def first(n, _):
        value = conv_tile(w_c, f_enc, n, cells, skip - 1)
        stack_tile(f_act, (value * jax.nn.sigmoid(value)).astype(jnp.bfloat16), n, rows)
        return 0

    lax.fori_loop(0, (thick + 2) * per_plane, first, 0)

    def second(n, _):
        value = conv_tile(w_d, f_act, n, cells)
        at = pl.ds(pl.multiple_of(n * TILE + thick * cells, TILE), TILE)
        base = f_enc[channels : 2 * channels, at].astype(jnp.float32)
        store_rows(out, (base + value).astype(jnp.bfloat16), n, rows)
        return 0

    lax.fori_loop(0, thick * per_plane, second, 0)


def flipped(index, bit):
    return index + (1 << bit) * (1 - 2 * lax.rem(index // (1 << bit), 2))


def crossed(left, right, bits):
    total = 0
    for bit in range(bits):
        one = lax.rem(left // (1 << bit), 2)
        two = lax.rem(right // (1 << bit), 2)
        total = total + (1 << bit) * (one + two - 2 * one * two)
    return total


def owner_kernel(
    replicas, slabs, scale,
    tensor_of, used, assignment, grads, first, second, master,
    params, out_first, out_second, out_master,
    work, landed, held, send_one, recv_one, send_two, recv_two,
):
    slots, taps, share = first.shape
    me, lane = lax.axis_index("dp"), lax.axis_index("space")
    dp_bits, space_bits = replicas.bit_length() - 1, slabs.bit_length() - 1
    core = lax.rem(me, 2)
    turn = [(k, (k + 1) % space_bits) for k in range(space_bits)]
    weight = [(1 - core) * (1 << one) + core * (1 << two) for one, two in turn]
    by_core = (flipped(me, 0), lane)
    by_space = [
        (me, (1 - core) * flipped(lane, one) + core * flipped(lane, two)) for one, two in turn
    ]
    by_dp = [(flipped(me, bit), lane) for bit in range(1, dp_bits)]

    barrier = pltpu.get_barrier_semaphore()
    for partner in [by_core] + by_space + by_dp:
        pl.semaphore_signal(
            barrier, inc=1, device_id=partner, device_id_type=pl.DeviceIdType.MESH
        )
    pl.semaphore_wait(barrier, dp_bits + space_bits)

    def build(odd):
        def one(n, _):
            apart = 2 * (n // slabs) + odd
            aside = lax.rem(n, slabs)
            owner = crossed(me, apart, dp_bits)
            column = crossed(lane, aside, space_bits)
            columns = pl.ds(pl.multiple_of(column * share, share), share)
            for slot in range(slots):
                number = owner * slots + slot
                value = grads[tensor_of[number], :, columns].astype(jnp.float32)
                work[apart * slabs + aside, slot] = (value * used[number]).astype(jnp.bfloat16)
            return 0

        lax.fori_loop(0, replicas * slabs // 2, one, 0)

    order = [by_core] + by_space + by_dp

    def place_of(chunk):
        core_bit, turns, rest = chunk[0], chunk[1 : 1 + space_bits], chunk[1 + space_bits :]
        apart = core_bit + sum(bit << (k + 1) for k, bit in enumerate(rest))
        index = apart * slabs
        for bit, amount in zip(turns, weight):
            index = index + amount * bit
        return index

    depth = dp_bits + space_bits
    half = replicas * slabs // 2

    def core_number(chunk):
        rest = sum(bit << k for k, bit in enumerate(chunk[1 + space_bits :]))
        index = rest * slabs
        for bit, amount in zip(chunk[1 : 1 + space_bits], weight):
            index = index + amount * bit
        return index

    def tails(length):
        out = [()]
        for _ in range(length):
            out = [(bit,) + tail for bit in (1, 0) for tail in out]
        return out

    numbers, count = {}, half
    for step in range(1, depth):
        for tail in tails(depth - 1 - step):
            numbers[(0,) * step + (1,) + tail] = count
            count += 1

    def number_of(chunk):
        return core_number(chunk) if chunk[0] else numbers[chunk]

    sent = []

    def send(chunk, step, source, target, send_sem, recv_sem, number):
        copy = pltpu.make_async_remote_copy(
            src_ref=source,
            dst_ref=target,
            send_sem=send_sem.at[number],
            recv_sem=recv_sem.at[number],
            device_id=order[step],
            device_id_type=pl.DeviceIdType.MESH,
        )
        copy.start()
        sent.append(copy)
        return copy

    def reduce_send(chunk, step):
        number = number_of(chunk)
        return send(
            chunk, step, work.at[place_of(chunk)], landed.at[number], send_one, recv_one, number
        )

    build(1)
    flying = {}
    for tail in tails(depth - 1):
        chunk = (1,) + tail
        flying[chunk] = reduce_send(chunk, 0)
    build(0)
    for step in range(depth):
        for tail in tails(depth - 1 - step):
            came = (0,) * step + (1,) + tail
            target = (0,) * (step + 1) + tail
            flying[came].wait_recv()
            at, number = place_of(target), number_of(came)
            total = work[at].astype(jnp.float32) + landed[number].astype(jnp.float32)
            work[at] = total.astype(jnp.bfloat16)
            if tail and tail[0]:
                flying[target] = reduce_send(target, step + 1)
    for copy in sent:
        copy.wait_send()

    owned = work[0].astype(jnp.float32) * scale
    new_first = 0.9 * first[...] + 0.1 * owned
    new_second = 0.999 * second[...] + 0.001 * owned * owned
    update = new_first / bias_one / (jnp.sqrt(new_second / bias_two) + epsilon)
    new_master = master[...] - learn_rate * (update + decay_rate * master[...])
    out_first[...] = new_first
    out_second[...] = new_second
    out_master[...] = new_master
    held[0] = new_master.astype(jnp.bfloat16)

    sent.clear()

    def spread(chunk, step):
        came = chunk[:step] + (1,) + chunk[step + 1 :]
        number = number_of(came)
        return send(
            came, step, held.at[place_of(chunk)], held.at[place_of(came)], send_two, recv_two, number
        )

    have, core_copies = [(0,) * depth], []
    core_copies.append(spread(have[0], 0))
    for step in range(depth - 1, 0, -1):
        copies = [spread(chunk, step) for chunk in have]
        came = [chunk[:step] + (1,) + chunk[step + 1 :] for chunk in have]
        for copy, chunk in zip(copies, came):
            copy.wait_recv()
            core_copies.append(spread(chunk, 0))
        have = have + came
    for copy in core_copies:
        copy.wait_recv()
    for copy in sent:
        copy.wait_send()

    for column in range(slabs):
        aside = crossed(lane, column, space_bits)

        def place(tensor, _, column=column, aside=aside):
            slot = assignment[tensor]
            apart = crossed(me, slot // slots, dp_bits)
            params[tensor, :, column * share : (column + 1) * share] = held[
                apart * slabs + aside, lax.rem(slot, slots)
            ]
            return 0

        lax.fori_loop(0, params.shape[0], place, 0)


def whole(count):
    return [pl.BlockSpec(memory_space=pltpu.VMEM)] * count


def stacked_weights(kernel, channels):
    taps = kernel.reshape(3, 3, 3, channels, channels)
    return taps.transpose(0, 2, 3, 1, 4).reshape(3, 3 * channels, 3 * channels)


def turned_weights(kernel, channels):
    taps = kernel.reshape(3, 3, 3, channels, channels)[::-1, ::-1, ::-1]
    return taps.transpose(0, 2, 4, 1, 3).reshape(3, 3 * channels, 3 * channels)


def unstacked(grad, channels):
    taps = grad.reshape(3, 3, channels, 3, channels).transpose(0, 3, 1, 2, 4)
    return taps.reshape(27, channels * channels)


def neighbours(field):
    count = lax.axis_size("space")
    forward = [(i, (i + 1) % count) for i in range(count)]
    backward = [(target, source) for source, target in forward]
    low = lax.ppermute(field, "space", forward)
    high = lax.ppermute(field, "space", backward)
    return low, field, high


def per_device(
    decoder_input,
    cotangent,
    encoder_input,
    decoder_weights,
    other_grads,
    assignment,
    moment_first,
    moment_second,
    master_weights,
):
    channels, thick, rows, lanes = decoder_input.shape[1:]
    replicas = lax.axis_size("dp")
    slabs = lax.axis_size("space")
    slots, taps, share = moment_first.shape
    tensors = assignment.shape[0]
    every_slot = replicas * slots
    cells = rows * lanes
    scale = 1.0 / math.sqrt(replicas * thick * slabs * cells)
    params = pltpu.CompilerParams(vmem_limit_bytes=48 * 1024 * 1024)

    dec = neighbours(decoder_input[0].transpose(1, 2, 0, 3))
    cot = neighbours(cotangent[0].transpose(1, 2, 0, 3))
    w_a = stacked_weights(decoder_weights[0], channels)
    w_at = turned_weights(decoder_weights[0], channels)
    w_bt = turned_weights(decoder_weights[1], channels)
    wide = 3 * channels
    field = jax.ShapeDtypeStruct((thick, rows, channels, lanes), jnp.bfloat16)
    small = jax.ShapeDtypeStruct((3, wide, wide), jnp.float32)
    bf = jnp.bfloat16
    conv_flops = 2 * 27 * channels * channels * cells
    input_grad, grad_a, grad_b = pl.pallas_call(
        functools.partial(decoder_kernel, rows),
        out_shape=(field, small, small),
        in_specs=whole(9),
        out_specs=tuple(whole(3)),
        scratch_shapes=[
            pltpu.VMEM((wide, 3 * thick * cells), bf),
            pltpu.VMEM((wide, 3 * thick * cells), bf),
            pltpu.VMEM((wide, (thick + 2) * cells), bf),
            pltpu.VMEM((wide, (thick + 2) * cells), bf),
            pltpu.VMEM((wide, thick * cells), bf),
            pltpu.VMEM((wide, thick * cells), bf),
        ],
        compiler_params=params,
        cost_estimate=pl.CostEstimate(
            flops=30 * conv_flops, bytes_accessed=8 * 2**20, transcendentals=0
        ),
        name="decoder",
    )(*dec, *cot, w_a, w_bt, w_at)
    input_grad = input_grad.transpose(2, 0, 1, 3)[None]

    pair = jnp.stack([unstacked(grad_a, channels), unstacked(grad_b, channels)])
    match = assignment[None, :] == jnp.arange(every_slot, dtype=jnp.int32)[:, None]
    used = jnp.any(match, axis=1).astype(jnp.float32)
    tensor_of = jnp.argmax(match, axis=1).astype(jnp.int32)
    mixed = (other_grads[0, 0, :2].astype(jnp.float32) + pair).astype(bf)
    grads = jnp.concatenate([mixed, other_grads[0, 0, 2:]], axis=0)
    chunks = replicas * slabs
    state = jax.ShapeDtypeStruct(moment_first.shape, jnp.float32)
    scalars = [pl.BlockSpec(memory_space=pltpu.SMEM)] * 3
    new_params, new_first, new_second, new_master = pl.pallas_call(
        functools.partial(owner_kernel, replicas, slabs, scale),
        out_shape=(
            jax.ShapeDtypeStruct((tensors, taps, slabs * share), bf),
            state,
            state,
            state,
        ),
        in_specs=scalars + whole(4),
        out_specs=tuple(whole(4)),
        scratch_shapes=[
            pltpu.VMEM((chunks, slots, taps, share), bf),
            pltpu.VMEM((chunks - 1, slots, taps, share), bf),
            pltpu.VMEM((chunks, slots, taps, share), bf),
        ]
        + [pltpu.SemaphoreType.DMA((chunks - 1,))] * 4,
        compiler_params=pltpu.CompilerParams(
            vmem_limit_bytes=56 * 1024 * 1024, collective_id=0, has_side_effects=True
        ),
        cost_estimate=pl.CostEstimate(
            flops=2**24, bytes_accessed=16 * 2**20, transcendentals=0
        ),
        name="owners",
    )(tensor_of, used, assignment, grads, moment_first, moment_second, master_weights)
    rest = new_params[2:4]

    enc = neighbours(encoder_input[0].transpose(1, 2, 0, 3))
    w_c = stacked_weights(rest[0], channels)
    w_d = stacked_weights(rest[1], channels)
    encoder_out = pl.pallas_call(
        functools.partial(encoder_kernel, rows),
        out_shape=field,
        in_specs=whole(5),
        out_specs=whole(1)[0],
        scratch_shapes=[
            pltpu.VMEM((wide, 3 * thick * cells), bf),
            pltpu.VMEM((wide, (thick + 2) * cells), bf),
        ],
        compiler_params=params,
        cost_estimate=pl.CostEstimate(
            flops=12 * conv_flops, bytes_accessed=4 * 2**20, transcendentals=0
        ),
        name="encoder",
    )(*enc, w_c, w_d)
    encoder_out = encoder_out.transpose(2, 0, 1, 3)[None]
    return (input_grad, encoder_out, new_params, new_first, new_second, new_master)


def solution(mesh):
    in_specs = (
        P("dp", None, "space", None, None),
        P("dp", None, "space", None, None),
        P("dp", None, "space", None, None),
        P(),
        P("dp", "space", None, None, None),
        P(),
        P("dp", None, "space"),
        P("dp", None, "space"),
        P("dp", None, "space"),
    )
    out_specs = (
        P("dp", None, "space", None, None),
        P("dp", None, "space", None, None),
        P(),
        P("dp", None, "space"),
        P("dp", None, "space"),
        P("dp", None, "space"),
    )
    return jax.shard_map(
        per_device, mesh=mesh, in_specs=in_specs, out_specs=out_specs, check_vma=False
    )
```
